128 devices in a mesh: role: 2 (over core), batch: 8 (over y_lo, x), tensor: 8 (over z, y_hi).
Axes of the slice: x: 4, y: 4 (y_hi: 2, y_lo: 2; y = y_hi * 2 + y_lo), z: 4, core: 2. Of those that a mesh axis runs over, the one named last changes fastest.
Arguments:
- queries: bfloat16 [128, 8192], P(('role', 'batch'), 'tensor'), may hold values from -200 to 200
- new_keys: bfloat16 [128, 1024], P(('role', 'batch'), 'tensor'), may hold values from -6 to 6
- new_values: bfloat16 [128, 1024], P(('role', 'batch'), 'tensor'), may hold values from -6 to 6
- key_cache: bfloat16 [128, 8, 3072, 128], P(('role', 'batch'), 'tensor'), may hold values from -6 to 6
- value_cache: bfloat16 [128, 8, 3072, 128], P(('role', 'batch'), 'tensor'), may hold values from -6 to 6
- lengths: int32 [128], P(('role', 'batch')), may hold values from 1 to 3072, as said below
- residual: bfloat16 [128, 8192], P(('role', 'batch'), 'tensor'), may hold values from -6 to 6
- norm_gain: bfloat16 [8192], replicated, may hold values from 0.25 to 1.75
- gate_weight: bfloat16 [8192, 28672], P(None, ('role', 'batch', 'tensor')), may hold values from -0.0625 to 0.0625
- up_weight: bfloat16 [8192, 28672], P(None, ('role', 'batch', 'tensor')), may hold values from -0.0625 to 0.0625
- down_weight: bfloat16 [28672, 8192], P(('role', 'batch', 'tensor')), may hold values from -0.125 to 0.125
Outputs:
- layer_out: bfloat16 [128, 8192], P(('role', 'batch'), 'tensor')
The draws below stay inside these ranges and needn't reach their ends.
Inputs may be any that keep to these rules, and one draw needn't show every extreme that they name: `lengths`: each row has 1 to 3072 cached tokens, and some row has exactly 3072.
All inputs are finite; a program needn't handle non-finite values.
Results may differ from the reference program's by a relative error of at most 0.0063.
Values may be sent and summed in bfloat16 or wider, within the bound.
No kernel may reach another device: no remote copies, remote signals or barrier semaphores. Data moves between devices by JAX's collectives and lax.ppermute only.
A program may use at most 128 MiB of HBM per device.

```python
import jax
import jax.numpy as jnp
from jax import lax

HD = 128
QPK = 8
KVH = 8
D = 8192
FF = 28672
L = 3072
ROWS_DEV = 8
ROWS = 128


def cached_keys(key):
    return jax.random.normal(key, (ROWS, KVH, L, HD), jnp.float32)


def draw_key_cache(key, part):
    shared = cached_keys(key)
    return jnp.clip(shared, -6.0, 6.0).astype(jnp.bfloat16)


def draw_queries(key, part):
    key = jax.random.fold_in(key, 2)
    fresh = jnp.clip(jax.random.normal(key, (ROWS, KVH, QPK, HD), jnp.float32), -6.0, 6.0)
    return fresh.reshape(ROWS, D).astype(jnp.bfloat16)


def draw_lengths(key, part):
    key = jax.random.fold_in(key, 3)
    row_index = jnp.arange(ROWS, dtype=jnp.int32)
    device_cap = L // (1 + row_index // ROWS_DEV % 4)
    drawn = jax.random.randint(key, (ROWS,), 1, device_cap + 1, dtype=jnp.int32)
    return drawn.at[0].set(L)


def strengthened(result, stream_key, source, target, shards_of, factor):
    owner, partner = [(jnp.arange(result.shape[dim]) // (result.shape[dim] // shards_of)).reshape([-1 if axis == dim else 1 for axis in range(result.ndim)]) for dim in (source, target)]
    chosen = jax.random.permutation(stream_key, shards_of)[partner]
    strong = (owner == chosen) | (owner == (partner + shards_of // 2) % shards_of)
    return jnp.where(strong, factor * result, result)


def block_levels(key, shape, shards, low, largest):
    level = 1.0
    for dim, shards_of in shards:
        heights = jax.random.uniform(jax.random.fold_in(jax.random.fold_in(key, 6), dim), (shards_of,), jnp.float32, low / len(shards), largest / len(shards))
        level = level * jnp.repeat(jnp.exp(heights), shape[dim] // shards_of).reshape((-1,) + (1,) * (len(shape) - 1 - dim))
    return level


def centred(stream_key, shape, deviation, most, pieces=(), kind=jnp.bfloat16):
    gain = block_levels(stream_key, shape, pieces, -0.22, 0.18) if pieces else 1.0
    values = jax.random.normal(stream_key, shape, jnp.float32) * deviation * gain
    return jnp.minimum(jnp.maximum(values, -most), most).astype(kind)


def gaussian_with(stream_key, shape, deviation, bound, split, heavy, kind=jnp.bfloat16):
    entries = deviation * jax.random.normal(stream_key, shape, jnp.float32)
    if split:
        entries = entries * block_levels(stream_key, shape, split, -0.22, 0.18)
    return jnp.clip(strengthened(entries, jax.random.fold_in(stream_key, 3), *heavy), -bound, bound).astype(kind)


def setup_inputs(seed: int = 0) -> dict:
    splits = jax.random.split(jax.random.key(seed), 12)
    queries = draw_queries(jax.random.fold_in(splits[11], 71), 0)
    new_keys = centred(splits[1], (ROWS, KVH * HD), 1.0, 6.0, ((0, 16), (1, 8)))
    new_values = centred(splits[2], (ROWS, KVH * HD), 1.0, 6.0, ((0, 16), (1, 8)))
    key_cache = draw_key_cache(jax.random.fold_in(splits[11], 71), 0)
    value_cache = centred(splits[4], (ROWS, KVH, L, HD), 1.0, 6.0, ((0, 16), (1, 8)))
    lengths = draw_lengths(jax.random.fold_in(splits[11], 71), 0)
    residual = centred(splits[6], (ROWS, D), 1.0, 6.0, ((0, 16), (1, 8)))
    norm_gain = jnp.clip(1.0 + 0.15 * jax.random.normal(splits[7], (D,), jnp.float32), 0.25, 1.75).astype(jnp.bfloat16)
    gate_weight = centred(splits[8], (D, FF), D ** -0.5, 0.0625, ((1, 128),))
    up_weight = centred(splits[9], (D, FF), D ** -0.5, 0.0625, ((1, 128),))
    down_weight = gaussian_with(splits[10], (FF, D), FF ** -0.5, 0.125, ((0, 128),), (0, 1, 128, 5.5))
    return {"queries": queries, "new_keys": new_keys, "new_values": new_values, "key_cache": key_cache, "value_cache": value_cache, "lengths": lengths, "residual": residual, "norm_gain": norm_gain, "gate_weight": gate_weight, "up_weight": up_weight, "down_weight": down_weight}


def attend_row(packed):
    query_row, keys_row, values_row, own_key, own_value, length = packed
    factor = HD ** (-0.5)
    scores = jnp.einsum('gqd,gtd->gqt', query_row, keys_row.astype(jnp.float32)) * factor
    position = jnp.arange(L)
    scores = jnp.where(position[None, None, :] < length, scores, -jnp.inf)
    own_score = jnp.einsum('gqd,gd->gq', query_row, own_key) * factor
    top_score = jnp.maximum(lax.optimization_barrier(jnp.max(scores, axis=-1)), own_score)
    weights = jnp.exp(scores - top_score[..., None])
    own_weight = jnp.exp(own_score - top_score)
    denominator = lax.optimization_barrier(jnp.sum(weights, axis=-1)) + own_weight
    weights_low = (weights / denominator[..., None]).astype(jnp.bfloat16)
    own_low = (own_weight / denominator).astype(jnp.bfloat16)
    mixed = jnp.einsum('gqt,gtd->gqd', weights_low.astype(jnp.float32), values_row.astype(jnp.float32))
    return mixed + own_low.astype(jnp.float32)[..., None] * own_value[:, None, :]

def reference(queries, new_keys, new_values, key_cache, value_cache, lengths, residual, norm_gain, gate_weight, up_weight, down_weight):
    total_rows = queries.shape[0]
    query_heads = queries.astype(jnp.float32).reshape(total_rows, KVH, QPK, HD)
    own_keys = new_keys.astype(jnp.float32).reshape(total_rows, KVH, HD)
    own_values = new_values.astype(jnp.float32).reshape(total_rows, KVH, HD)
    attended = lax.map(attend_row, (query_heads, key_cache, value_cache, own_keys, own_values, lengths))
    attended = attended.reshape(total_rows, D)
    hidden_state = (residual.astype(jnp.float32) + attended).astype(jnp.bfloat16)
    wide = hidden_state.astype(jnp.float32)
    mean_square = lax.optimization_barrier(jnp.mean(wide * wide, axis=-1, keepdims=True))
    normed = (wide * lax.rsqrt(mean_square + 1e-05) * norm_gain.astype(jnp.float32)).astype(jnp.bfloat16)
    gate = jnp.dot(normed, gate_weight, preferred_element_type=jnp.float32)
    up_part = jnp.dot(normed, up_weight, preferred_element_type=jnp.float32)
    activation = (jax.nn.silu(gate) * up_part).astype(jnp.bfloat16)
    ffn_out = jnp.dot(activation, down_weight, preferred_element_type=jnp.float32)
    return (wide + ffn_out).astype(jnp.bfloat16)
```

```python
import jax
import jax.numpy as jnp
from jax import lax
from jax.sharding import PartitionSpec as P

AXES = ("role", "batch", "tensor")
CHIPS = ("batch", "tensor")


def local(
    queries,
    new_keys,
    new_values,
    key_cache,
    value_cache,
    lengths,
    residual,
    norm_gain,
    gate_weight,
    up_weight,
    down_weight,
):
    local_rows = queries.shape[0]
    head_size = new_keys.shape[1]
    group_heads = queries.shape[1] // head_size
    cache_len = key_cache.shape[2]
    width = queries.shape[1]
    batch = lax.axis_size("batch")
    tensor = lax.axis_size("tensor")
    chips = batch * tensor
    swap = [(0, 1), (1, 0)]
    gates = (gate_weight, lax.ppermute(gate_weight, "role", swap))
    ups = (up_weight, lax.ppermute(up_weight, "role", swap))
    downs = (down_weight, lax.ppermute(down_weight, "role", swap))

    factor = head_size ** (-0.5)
    query_heads = queries.reshape(local_rows, group_heads, head_size)
    cache_keys = key_cache.reshape(local_rows, cache_len, head_size)
    cache_values = value_cache.reshape(local_rows, cache_len, head_size)
    scores = (
        jnp.einsum("rqd,rtd->rqt", query_heads, cache_keys, preferred_element_type=jnp.float32)
        * factor
    )
    position = jnp.arange(cache_len)
    scores = jnp.where(position[None, None, :] < lengths[:, None, None], scores, -jnp.inf)
    own_score = (
        jnp.einsum("rqd,rd->rq", query_heads, new_keys, preferred_element_type=jnp.float32) * factor
    )
    top_score = jnp.maximum(jnp.max(scores, axis=-1), own_score)
    weights = jnp.exp(scores - top_score[..., None])
    own_weight = jnp.exp(own_score - top_score)
    denominator = jnp.sum(weights, axis=-1) + own_weight
    weights_low = (weights / denominator[..., None]).astype(jnp.bfloat16)
    own_low = (own_weight / denominator).astype(jnp.bfloat16)
    mixed = jnp.einsum(
        "rqt,rtd->rqd", weights_low, cache_values, preferred_element_type=jnp.float32
    )
    mixed = (
        mixed + own_low.astype(jnp.float32)[..., None] * new_values.astype(jnp.float32)[:, None, :]
    )
    attended = mixed.reshape(local_rows, width)
    hidden_state = (residual.astype(jnp.float32) + attended).astype(jnp.bfloat16)

    copies = jnp.broadcast_to(hidden_state[None], (chips, local_rows, width))
    pieces = lax.all_to_all(copies, CHIPS, 0, 0, tiled=True)
    all_hidden = (
        pieces.reshape(batch, tensor, local_rows, width)
        .transpose(0, 2, 1, 3)
        .reshape(batch * local_rows, tensor * width)
    )
    wide = all_hidden.astype(jnp.float32)
    mean_square = jnp.mean(wide * wide, axis=-1, keepdims=True)
    normed = (wide * lax.rsqrt(mean_square + 1e-05) * norm_gain.astype(jnp.float32)).astype(
        jnp.bfloat16
    )
    partial_out = 0.0
    for gate_part, up_part, down_part in zip(gates, ups, downs):
        gate = jnp.dot(normed, gate_part, preferred_element_type=jnp.float32)
        up = jnp.dot(normed, up_part, preferred_element_type=jnp.float32)
        activation = (jax.nn.silu(gate) * up).astype(jnp.bfloat16)
        partial_out += jnp.dot(activation, down_part, preferred_element_type=jnp.float32)
    sent = (
        partial_out.astype(jnp.bfloat16)
        .reshape(batch, local_rows, tensor, width)
        .transpose(0, 2, 1, 3)
        .reshape(chips, local_rows, width)
    )
    received = lax.all_to_all(sent, CHIPS, 0, 0, tiled=True)
    summed = jnp.sum(received.astype(jnp.float32), axis=0)
    return (hidden_state.astype(jnp.float32) + summed).astype(jnp.bfloat16)


def solution(mesh):
    rows = ("role", "batch")
    in_specs = (
        P(rows, "tensor"),
        P(rows, "tensor"),
        P(rows, "tensor"),
        P(rows, "tensor", None, None),
        P(rows, "tensor", None, None),
        P(rows),
        P(rows, "tensor"),
        P(),
        P(None, AXES),
        P(None, AXES),
        P(AXES, None),
    )
    return jax.shard_map(
        local, mesh=mesh, in_specs=in_specs, out_specs=P(rows, "tensor"), check_vma=False
    )
```

```python
import functools

import jax
import jax.numpy as jnp
from jax import lax
from jax.experimental import pallas as pl
from jax.experimental.pallas import tpu as pltpu
from jax.sharding import PartitionSpec as P

AXES = ("role", "batch", "tensor")
CHIPS = ("batch", "tensor")
CHUNK = 1024
TOGETHER = 4
STEP = 2048
CONTRACT_LAST = (((1,), (1,)), ((), ()))
F32 = jnp.float32
BF16 = jnp.bfloat16
HBM = pl.BlockSpec(memory_space=pltpu.HBM)
VMEM = pl.BlockSpec(memory_space=pltpu.VMEM)


def in_hbm(array):
    return pltpu.with_memory_space_constraint(array, pltpu.HBM)


def attention_kernel(
    lengths_hbm,
    queries_hbm,
    new_keys_hbm,
    new_values_hbm,
    residual_hbm,
    keys_hbm,
    values_hbm,
    hidden_out,
    copies_out,
    lengths,
    queries,
    new_keys,
    new_values,
    residual,
    keys,
    values,
    heads,
    probs,
    mixed,
    small_sems,
    sems,
):
    rows, group, head = heads.shape
    cache_len = keys.shape[1]
    chunks = cache_len // CHUNK
    copies = copies_out.shape[0]

    def copy(which, row, chunk):
        source, target = ((keys_hbm, keys), (values_hbm, values))[which]
        span = pl.ds(chunk * CHUNK, CHUNK)
        return pltpu.make_async_copy(
            source.at[row, 0, span], target.at[row, span], sems.at[which, row, chunk]
        )

    def used(row, chunk):
        return chunk * CHUNK < lengths[row]

    small = [
        pltpu.make_async_copy(source, target, small_sems.at[i])
        for i, (source, target) in enumerate(
            (
                (lengths_hbm, lengths),
                (queries_hbm, queries),
                (new_keys_hbm, new_keys),
                (new_values_hbm, new_values),
                (residual_hbm, residual),
            )
        )
    ]
    for one in small:
        one.start()
    for which in range(2):
        for row in range(rows):
            copy(which, row, 0).start()
    small[0].wait()
    for which in range(2):
        for row in range(rows):
            for chunk in range(1, chunks):

                @pl.when(used(row, chunk))
                def _():
                    copy(which, row, chunk).start()

    for one in small[1:]:
        one.wait()

    def arrive(which, first):
        for row in range(first, first + TOGETHER):
            copy(which, row, 0).wait()
            for chunk in range(1, chunks):

                @pl.when(used(row, chunk))
                def _():
                    copy(which, row, chunk).wait()

    factor = head ** (-0.5)
    for j in range(group):
        heads[:, j, :] = queries[:, j * head : (j + 1) * head].astype(F32)
    own_scores = (
        jnp.sum(heads[...] * new_keys[...].astype(F32)[:, None, :], axis=-1, keepdims=True)
        * factor
    )
    place = lax.broadcasted_iota(jnp.int32, (group, cache_len), 1)
    own_probs = []
    for first in range(0, rows, TOGETHER):
        arrive(0, first)
        for row in range(first, first + TOGETHER):
            products = lax.dot_general(
                heads[row].astype(BF16), keys[row], CONTRACT_LAST, preferred_element_type=F32
            )
            scores = jnp.where(place < lengths[row], products * factor, -jnp.inf)
            own = own_scores[row]
            top = jnp.maximum(jnp.max(scores, axis=-1, keepdims=True), own)
            weights = jnp.exp(scores - top)
            own_weight = jnp.exp(own - top)
            denominator = jnp.sum(weights, axis=-1, keepdims=True) + own_weight
            probs[row] = (weights / denominator).astype(BF16)
            own_probs.append((own_weight / denominator).astype(BF16).astype(F32))

    for first in range(0, rows, TOGETHER):
        arrive(1, first)
        for row in range(first, first + TOGETHER):
            total = own_probs[row] * new_values[row : row + 1, :].astype(F32)
            for chunk in range(chunks):
                span = slice(chunk * CHUNK, (chunk + 1) * CHUNK)
                part = values[row, span, :]
                if chunk:
                    part = jnp.where(used(row, chunk), part, jnp.zeros_like(part))
                total += jnp.dot(probs[row, :, span], part, preferred_element_type=F32)
            mixed[row] = total

    for j in range(group):
        span = slice(j * head, (j + 1) * head)
        hidden = (residual[:, span].astype(F32) + mixed[:, j, :]).astype(BF16)
        hidden_out[:, span] = hidden
        for k in range(copies):
            copies_out[k, :, span] = hidden


def attention(queries, new_keys, new_values, key_cache, value_cache, lengths, residual, copies):
    rows, width = queries.shape
    head = new_keys.shape[1]
    group = width // head
    cache_len = key_cache.shape[2]
    operands = (lengths, queries, new_keys, new_values, residual, key_cache, value_cache)
    return pl.pallas_call(
        attention_kernel,
        out_shape=(
            jax.ShapeDtypeStruct((rows, width), BF16),
            jax.ShapeDtypeStruct((copies, rows, width), BF16),
        ),
        in_specs=[HBM] * len(operands),
        out_specs=(VMEM, VMEM),
        scratch_shapes=[
            pltpu.SMEM((rows,), jnp.int32),
            pltpu.VMEM((rows, width), BF16),
            pltpu.VMEM((rows, head), BF16),
            pltpu.VMEM((rows, head), BF16),
            pltpu.VMEM((rows, width), BF16),
            pltpu.VMEM((rows, cache_len, head), BF16),
            pltpu.VMEM((rows, cache_len, head), BF16),
            pltpu.VMEM((rows, group, head), F32),
            pltpu.VMEM((rows, group, cache_len), BF16),
            pltpu.VMEM((rows, group, head), F32),
            pltpu.SemaphoreType.DMA((5,)),
            pltpu.SemaphoreType.DMA((2, rows, cache_len // CHUNK)),
        ],
        compiler_params=pltpu.CompilerParams(vmem_limit_bytes=24 << 20),
        cost_estimate=pl.CostEstimate(
            flops=4 * rows * group * cache_len * head,
            bytes_accessed=4 * rows * cache_len * head,
            transcendentals=rows * group * cache_len,
        ),
        name="attention",
    )(*(in_hbm(x) for x in operands))


def feed_forward_kernel(batch, tensor, pieces, gain, *refs):
    mate = refs[:3]
    own_hbm = refs[3:6]
    out, normed = refs[6:8]
    own = refs[8:11]
    sems = refs[11]
    rows, width = pieces.shape[1:]
    units, features = own[0].shape
    steps = features // STEP

    def span_of(step):
        return slice(step * STEP, (step + 1) * STEP)

    arrivals = []
    for which in ((0, 1), (2,)):
        for step in range(steps):
            arrivals.append(
                [
                    pltpu.make_async_copy(
                        own_hbm[w].at[:, span_of(step)],
                        own[w].at[:, span_of(step)],
                        sems.at[w, step],
                    )
                    for w in which
                ]
            )
    for group in arrivals:
        for one in group:
            one.start()

    for pair in range(batch // 2):
        inverse = []
        for half in range(2):
            start = (pair * 2 + half) * tensor
            total = jnp.zeros((rows, width), F32)
            for t in range(tensor):
                part = pieces[start + t].astype(F32)
                total = total + part * part
            mean_square = jnp.sum(total, axis=-1, keepdims=True) * (1.0 / features)
            inverse.append(lax.rsqrt(mean_square + 1e-05))
        for t in range(tensor):
            lanes = gain.shape[1]
            tiles = width // lanes
            scale = jnp.concatenate(
                [gain[t * tiles + i : t * tiles + i + 1, :].astype(F32) for i in range(tiles)],
                axis=1,
            )
            parts = [
                pieces[(pair * 2 + half) * tensor + t].astype(F32) * inverse[half] * scale
                for half in range(2)
            ]
            normed[pair * 2 * rows : (pair + 1) * 2 * rows, t * width : (t + 1) * width] = (
                jnp.concatenate(parts, axis=0).astype(BF16)
            )

    def project(weights, arrived):
        sums = [jnp.zeros((units, batch * rows), F32) for _ in range(2)]
        for step in range(steps):
            for one in arrived[step]:
                one.wait()
            block = normed[:, span_of(step)]
            for i in range(2):
                sums[i] += lax.dot_general(
                    weights[i][:, span_of(step)],
                    block,
                    CONTRACT_LAST,
                    preferred_element_type=F32,
                )
        gate, up = sums
        return (gate / (1.0 + jnp.exp(-gate)) * up).astype(BF16).T

    active_mate = project(mate, [()] * steps)
    active_own = project(own, arrivals[:steps])
    for step in range(steps):
        span = span_of(step)
        partial = jnp.dot(active_mate, mate[2][:, span], preferred_element_type=F32)
        for one in arrivals[steps + step]:
            one.wait()
        partial += jnp.dot(active_own, own[2][:, span], preferred_element_type=F32)
        for i in range(STEP // width):
            t = step * (STEP // width) + i
            for b in range(batch):
                out[b * tensor + t] = partial[
                    b * rows : (b + 1) * rows, i * width : (i + 1) * width
                ].astype(BF16)


def feed_forward(pieces, gain, own, mate, batch, tensor):
    rows, width = pieces.shape[1:]
    features = tensor * width
    units = own[2].shape[0]
    own = [in_hbm(w) for w in (own[0].T, own[1].T, own[2])]
    mate = [mate[0].T, mate[1].T, mate[2]]
    return pl.pallas_call(
        functools.partial(feed_forward_kernel, batch, tensor),
        out_shape=jax.ShapeDtypeStruct(pieces.shape, BF16),
        in_specs=[VMEM] * 5 + [HBM] * 3,
        out_specs=VMEM,
        scratch_shapes=[pltpu.VMEM((batch * rows, features), BF16)]
        + [pltpu.VMEM((units, features), BF16)] * 3
        + [pltpu.SemaphoreType.DMA((3, features // STEP))],
        compiler_params=pltpu.CompilerParams(vmem_limit_bytes=24 << 20),
        cost_estimate=pl.CostEstimate(
            flops=12 * batch * rows * units * features,
            bytes_accessed=12 * units * features,
            transcendentals=2 * batch * rows * units,
        ),
        name="feed_forward",
    )(pieces, gain.reshape(features // 128, 128), *mate, *own)


def local(
    queries,
    new_keys,
    new_values,
    key_cache,
    value_cache,
    lengths,
    residual,
    norm_gain,
    gate_weight,
    up_weight,
    down_weight,
):
    batch = lax.axis_size("batch")
    tensor = lax.axis_size("tensor")
    own = (gate_weight, up_weight, down_weight)
    mate = tuple(lax.ppermute(w, "role", [(0, 1), (1, 0)]) for w in own)
    hidden_state, copies = attention(
        queries, new_keys, new_values, key_cache, value_cache, lengths, residual, batch * tensor
    )
    pieces = lax.all_to_all(copies, CHIPS, 0, 0, tiled=True)
    partial_out = feed_forward(pieces, norm_gain, own, mate, batch, tensor)
    received = lax.all_to_all(partial_out, CHIPS, 0, 0, tiled=True)
    summed = jnp.sum(received.astype(F32), axis=0)
    return (hidden_state.astype(F32) + summed).astype(BF16)


def solution(mesh):
    rows = ("role", "batch")
    in_specs = (
        P(rows, "tensor"),
        P(rows, "tensor"),
        P(rows, "tensor"),
        P(rows, "tensor", None, None),
        P(rows, "tensor", None, None),
        P(rows),
        P(rows, "tensor"),
        P(),
        P(None, AXES),
        P(None, AXES),
        P(AXES, None),
    )
    return jax.shard_map(
        local, mesh=mesh, in_specs=in_specs, out_specs=P(rows, "tensor"), check_vma=False
    )
```

```python
import functools

import jax
import jax.numpy as jnp
from jax import lax
from jax.experimental import pallas as pl
from jax.experimental.pallas import tpu as pltpu
from jax.sharding import PartitionSpec as P

AXES = ("role", "batch", "tensor")
CHIPS = ("batch", "tensor")
PACK = 16
TOGETHER = 4
STAGE_AFTER = 0
STEP = 4096
CONTRACT_LAST = (((1,), (1,)), ((), ()))
F32 = jnp.float32
BF16 = jnp.bfloat16
HBM = pl.BlockSpec(memory_space=pltpu.HBM)
VMEM = pl.BlockSpec(memory_space=pltpu.VMEM)


def in_hbm(array):
    return pltpu.with_memory_space_constraint(array, pltpu.HBM)


def attention_kernel(
    lengths_hbm,
    queries_hbm,
    new_keys_hbm,
    new_values_hbm,
    residual_hbm,
    keys_hbm,
    values_hbm,
    gate_hbm,
    up_hbm,
    hidden_out,
    copies_out,
    gate_out,
    up_out,
    lengths,
    queries,
    new_keys,
    new_values,
    residual,
    keys,
    values,
    heads,
    probs,
    mixed,
    small_sems,
    sems,
    stage_sems,
):
    rows, group, head = heads.shape
    cache_len = keys.shape[1]
    copies = copies_out.shape[0]

    def copy(which, row):
        source, target = ((keys_hbm, keys), (values_hbm, values))[which]
        length = (lengths[row] + PACK - 1) // PACK * PACK
        span = pl.ds(0, pl.multiple_of(length, PACK))
        return pltpu.make_async_copy(
            source.at[row, 0, span], target.at[row, span], sems.at[which, row]
        )

    small = [
        pltpu.make_async_copy(source, target, small_sems.at[i])
        for i, (source, target) in enumerate(
            (
                (lengths_hbm, lengths),
                (queries_hbm, queries),
                (new_keys_hbm, new_keys),
                (new_values_hbm, new_values),
                (residual_hbm, residual),
            )
        )
    ]
    for one in small:
        one.start()
    for row in range(rows):
        values[row] = jnp.zeros((cache_len, head), BF16)
    small[0].wait()
    for which in range(2):
        for row in range(rows):
            copy(which, row).start()
    for one in small[1:]:
        one.wait()

    staged = [
        pltpu.make_async_copy(gate_hbm, gate_out, stage_sems.at[0]),
        pltpu.make_async_copy(up_hbm, up_out, stage_sems.at[1]),
    ]
    factor = head ** (-0.5)
    for j in range(group):
        heads[:, j, :] = queries[:, j * head : (j + 1) * head].astype(F32)
    own_scores = (
        jnp.sum(heads[...] * new_keys[...].astype(F32)[:, None, :], axis=-1, keepdims=True)
        * factor
    )
    place = lax.broadcasted_iota(jnp.int32, (group, cache_len), 1)
    own_probs = []
    for first in range(0, rows, TOGETHER):
        for row in range(first, first + TOGETHER):
            copy(0, row).wait()
        if first == STAGE_AFTER:
            for one in staged:
                one.start()
        for row in range(first, first + TOGETHER):
            products = lax.dot_general(
                heads[row].astype(BF16), keys[row], CONTRACT_LAST, preferred_element_type=F32
            )
            scores = jnp.where(place < lengths[row], products * factor, -jnp.inf)
            own = own_scores[row]
            top = jnp.maximum(jnp.max(scores, axis=-1, keepdims=True), own)
            weights = jnp.exp(scores - top)
            own_weight = jnp.exp(own - top)
            denominator = jnp.sum(weights, axis=-1, keepdims=True) + own_weight
            probs[row] = (weights / denominator).astype(BF16)
            own_probs.append((own_weight / denominator).astype(BF16).astype(F32))

    for first in range(0, rows, TOGETHER):
        for row in range(first, first + TOGETHER):
            copy(1, row).wait()
        for row in range(first, first + TOGETHER):
            total = own_probs[row] * new_values[row : row + 1, :].astype(F32)
            total += jnp.dot(probs[row], values[row], preferred_element_type=F32)
            mixed[row] = total

    for j in range(group):
        span = slice(j * head, (j + 1) * head)
        hidden = (residual[:, span].astype(F32) + mixed[:, j, :]).astype(BF16)
        hidden_out[:, span] = hidden
        for k in range(copies):
            copies_out[k, :, span] = hidden
    for one in staged:
        one.wait()


def attention(
    queries,
    new_keys,
    new_values,
    key_cache,
    value_cache,
    lengths,
    residual,
    copies,
    gate,
    up,
):
    rows, width = queries.shape
    head = new_keys.shape[1]
    group = width // head
    cache_len = key_cache.shape[2]
    operands = (
        lengths,
        queries,
        new_keys,
        new_values,
        residual,
        key_cache,
        value_cache,
        gate,
        up,
    )
    return pl.pallas_call(
        attention_kernel,
        out_shape=(
            jax.ShapeDtypeStruct((rows, width), BF16),
            jax.ShapeDtypeStruct((copies, rows, width), BF16),
            jax.ShapeDtypeStruct(gate.shape, BF16),
            jax.ShapeDtypeStruct(up.shape, BF16),
        ),
        in_specs=[HBM] * len(operands),
        out_specs=(VMEM,) * 4,
        scratch_shapes=[
            pltpu.SMEM((rows,), jnp.int32),
            pltpu.VMEM((rows, width), BF16),
            pltpu.VMEM((rows, head), BF16),
            pltpu.VMEM((rows, head), BF16),
            pltpu.VMEM((rows, width), BF16),
            pltpu.VMEM((rows, cache_len, head), BF16),
            pltpu.VMEM((rows, cache_len, head), BF16),
            pltpu.VMEM((rows, group, head), F32),
            pltpu.VMEM((rows, group, cache_len), BF16),
            pltpu.VMEM((rows, group, head), F32),
            pltpu.SemaphoreType.DMA((5,)),
            pltpu.SemaphoreType.DMA((2, rows)),
            pltpu.SemaphoreType.DMA((2,)),
        ],
        compiler_params=pltpu.CompilerParams(vmem_limit_bytes=24 << 20),
        cost_estimate=pl.CostEstimate(
            flops=4 * rows * group * cache_len * head,
            bytes_accessed=4 * rows * cache_len * head,
            transcendentals=rows * group * cache_len,
        ),
        name="attention",
    )(*(in_hbm(x) for x in operands))


def feed_forward_kernel(batch, tensor, place, pieces, gain, *refs):
    mate, (own_gate, own_up, down_hbm) = refs[:3], refs[3:6]
    out, normed, own_down, sems = refs[6:]
    rows, width = pieces.shape[1:]
    units, features = own_gate.shape
    arrivals = []
    for i, start in enumerate(range(0, features, STEP)):
        span = pl.ds(start, STEP)
        arrivals.append(
            pltpu.make_async_copy(down_hbm.at[:, span], own_down.at[:, span], sems.at[i])
        )
        arrivals[-1].start()
    lanes = gain.shape[1]
    tiles = width // lanes

    for pair in range(batch // 2):
        inverse = []
        for half in range(2):
            total = jnp.zeros((rows, width), F32)
            for t in range(tensor):
                part = pieces[place[(pair * 2 + half) * tensor + t]].astype(F32)
                total = total + part * part
            mean_square = jnp.sum(total, axis=-1, keepdims=True) * (1.0 / features)
            inverse.append(lax.rsqrt(mean_square + 1e-05))
        for t in range(tensor):
            scale = jnp.concatenate(
                [gain[t * tiles + i : t * tiles + i + 1, :].astype(F32) for i in range(tiles)],
                axis=1,
            )
            parts = [
                pieces[place[(pair * 2 + half) * tensor + t]].astype(F32) * inverse[half] * scale
                for half in range(2)
            ]
            normed[pair * 2 * rows : (pair + 1) * 2 * rows, t * width : (t + 1) * width] = (
                jnp.concatenate(parts, axis=0).astype(BF16)
            )

    def project(weights):
        sums = [jnp.zeros((units, batch * rows), F32) for _ in range(2)]
        for start in range(0, features, STEP):
            span = slice(start, start + STEP)
            block = normed[:, span]
            for i in range(2):
                sums[i] += lax.dot_general(
                    weights[i][:, span], block, CONTRACT_LAST, preferred_element_type=F32
                )
        gate, up = sums
        return (gate / (1.0 + jnp.exp(-gate)) * up).astype(BF16).T

    active_own = project((own_gate, own_up))
    active_mate = project(mate[:2])
    for one, start in zip(arrivals, range(0, features, STEP)):
        span = slice(start, start + STEP)
        partial = jnp.dot(active_mate, mate[2][:, span], preferred_element_type=F32)
        one.wait()
        partial += jnp.dot(active_own, own_down[:, span], preferred_element_type=F32)
        for i in range(STEP // width):
            t = start // width + i
            for b in range(batch):
                out[place[b * tensor + t]] = partial[
                    b * rows : (b + 1) * rows, i * width : (i + 1) * width
                ].astype(BF16)


def feed_forward(pieces, gain, own, mate, batch, tensor, place):
    rows, width = pieces.shape[1:]
    features = tensor * width
    units = own[2].shape[0]
    return pl.pallas_call(
        functools.partial(feed_forward_kernel, batch, tensor, place),
        out_shape=jax.ShapeDtypeStruct(pieces.shape, BF16),
        in_specs=[VMEM] * 7 + [HBM],
        out_specs=VMEM,
        scratch_shapes=[
            pltpu.VMEM((batch * rows, features), BF16),
            pltpu.VMEM((units, features), BF16),
            pltpu.SemaphoreType.DMA((features // STEP,)),
        ],
        compiler_params=pltpu.CompilerParams(vmem_limit_bytes=16 << 20),
        cost_estimate=pl.CostEstimate(
            flops=12 * batch * rows * units * features,
            bytes_accessed=12 * units * features,
            transcendentals=2 * batch * rows * units,
        ),
        name="feed_forward",
    )(pieces, gain.reshape(features // 128, 128), *mate, own[0], own[1], in_hbm(own[2]))


def chip_order(batch, tensor):
    side = round((batch * tensor) ** (1 / 3))
    order = []
    for step in range(batch * tensor):
        at = 21 * step % (batch * tensor)
        x, y, z = at % side, at // side % side, at // (side * side)
        half = side // 2
        order.append((y % half * side + x) * tensor + z * half + y // half)
    return order


def local(
    queries,
    new_keys,
    new_values,
    key_cache,
    value_cache,
    lengths,
    residual,
    norm_gain,
    gate_weight,
    up_weight,
    down_weight,
):
    batch = lax.axis_size("batch")
    tensor = lax.axis_size("tensor")
    chips = batch * tensor
    order = chip_order(batch, tensor)
    place = [order.index(chip) for chip in range(chips)]
    groups = [[role * chips + chip for chip in order] for role in range(2)]
    exchange = functools.partial(
        lax.all_to_all,
        axis_name=AXES,
        split_axis=0,
        concat_axis=0,
        tiled=True,
        axis_index_groups=groups,
    )
    own = (gate_weight.T, up_weight.T, down_weight)
    mate = tuple(lax.ppermute(w, "role", [(0, 1), (1, 0)]) for w in own)
    hidden_state, copies, *near = attention(
        queries,
        new_keys,
        new_values,
        key_cache,
        value_cache,
        lengths,
        residual,
        chips,
        own[0],
        own[1],
    )
    pieces = exchange(copies)
    own = (*near, own[2])
    partial_out = feed_forward(pieces, norm_gain, own, mate, batch, tensor, place)
    received = exchange(partial_out)
    summed = jnp.sum(received.astype(F32), axis=0)
    return (hidden_state.astype(F32) + summed).astype(BF16)


def solution(mesh):
    rows = ("role", "batch")
    in_specs = (
        P(rows, "tensor"),
        P(rows, "tensor"),
        P(rows, "tensor"),
        P(rows, "tensor", None, None),
        P(rows, "tensor", None, None),
        P(rows),
        P(rows, "tensor"),
        P(),
        P(None, AXES),
        P(None, AXES),
        P(AXES, None),
    )
    return jax.shard_map(
        local, mesh=mesh, in_specs=in_specs, out_specs=P(rows, "tensor"), check_vma=False
    )
```

```python
import functools

import jax
import jax.numpy as jnp
from jax import lax
from jax.experimental import pallas as pl
from jax.experimental.pallas import tpu as pltpu
from jax.sharding import PartitionSpec as P

AXES = ("role", "batch", "tensor")
CHIPS = ("batch", "tensor")
PACK = 16
TOGETHER = 4
STAGE_AFTER = 0
STEP = 4096
CONTRACT_LAST = (((1,), (1,)), ((), ()))
F32 = jnp.float32
BF16 = jnp.bfloat16
HBM = pl.BlockSpec(memory_space=pltpu.HBM)
VMEM = pl.BlockSpec(memory_space=pltpu.VMEM)


def in_hbm(array):
    return pltpu.with_memory_space_constraint(array, pltpu.HBM)


def attention_kernel(
    lengths_hbm,
    queries_hbm,
    new_keys_hbm,
    new_values_hbm,
    residual_hbm,
    keys_hbm,
    values_hbm,
    gate_hbm,
    up_hbm,
    hidden_out,
    copies_out,
    gate_out,
    up_out,
    lengths,
    queries,
    new_keys,
    new_values,
    residual,
    keys,
    values,
    heads,
    probs,
    mixed,
    small_sems,
    sems,
    stage_sems,
):
    rows, group, head = heads.shape
    cache_len = keys.shape[1]
    copies = copies_out.shape[0]

    def copy(which, row):
        source, target = ((keys_hbm, keys), (values_hbm, values))[which]
        length = (lengths[row] + PACK - 1) // PACK * PACK
        span = pl.ds(0, pl.multiple_of(length, PACK))
        return pltpu.make_async_copy(
            source.at[row, 0, span], target.at[row, span], sems.at[which, row]
        )

    small = [
        pltpu.make_async_copy(source, target, small_sems.at[i])
        for i, (source, target) in enumerate(
            (
                (lengths_hbm, lengths),
                (queries_hbm, queries),
                (new_keys_hbm, new_keys),
                (new_values_hbm, new_values),
                (residual_hbm, residual),
            )
        )
    ]
    for one in small:
        one.start()
    for row in range(rows):
        values[row] = jnp.zeros((cache_len, head), BF16)
    small[0].wait()
    for which in range(2):
        for row in range(rows):
            copy(which, row).start()
    for one in small[1:]:
        one.wait()

    staged = [
        pltpu.make_async_copy(gate_hbm, gate_out, stage_sems.at[0]),
        pltpu.make_async_copy(up_hbm, up_out, stage_sems.at[1]),
    ]
    factor = head ** (-0.5)
    for j in range(group):
        heads[:, j, :] = queries[:, j * head : (j + 1) * head].astype(F32)
    own_scores = (
        jnp.sum(heads[...] * new_keys[...].astype(F32)[:, None, :], axis=-1, keepdims=True)
        * factor
    )
    place = lax.broadcasted_iota(jnp.int32, (group, cache_len), 1)
    own_probs = []
    for first in range(0, rows, TOGETHER):
        for row in range(first, first + TOGETHER):
            copy(0, row).wait()
        if first == STAGE_AFTER:
            for one in staged:
                one.start()
        for row in range(first, first + TOGETHER):
            products = lax.dot_general(
                heads[row].astype(BF16), keys[row], CONTRACT_LAST, preferred_element_type=F32
            )
            scores = jnp.where(place < lengths[row], products * factor, -jnp.inf)
            own = own_scores[row]
            top = jnp.maximum(jnp.max(scores, axis=-1, keepdims=True), own)
            weights = jnp.exp(scores - top)
            own_weight = jnp.exp(own - top)
            denominator = jnp.sum(weights, axis=-1, keepdims=True) + own_weight
            probs[row] = (weights / denominator).astype(BF16)
            own_probs.append((own_weight / denominator).astype(BF16).astype(F32))

    for first in range(0, rows, TOGETHER):
        for row in range(first, first + TOGETHER):
            copy(1, row).wait()
        for row in range(first, first + TOGETHER):
            total = own_probs[row] * new_values[row : row + 1, :].astype(F32)
            total += jnp.dot(probs[row], values[row], preferred_element_type=F32)
            mixed[row] = total

    for j in range(group):
        span = slice(j * head, (j + 1) * head)
        hidden = (residual[:, span].astype(F32) + mixed[:, j, :]).astype(BF16)
        hidden_out[:, span] = hidden
        for k in range(copies):
            copies_out[k, :, span] = hidden
    for one in staged:
        one.wait()


def attention(
    queries,
    new_keys,
    new_values,
    key_cache,
    value_cache,
    lengths,
    residual,
    copies,
    gate,
    up,
):
    rows, width = queries.shape
    head = new_keys.shape[1]
    group = width // head
    cache_len = key_cache.shape[2]
    operands = (
        lengths,
        queries,
        new_keys,
        new_values,
        residual,
        key_cache,
        value_cache,
        gate,
        up,
    )
    return pl.pallas_call(
        attention_kernel,
        out_shape=(
            jax.ShapeDtypeStruct((rows, width), BF16),
            jax.ShapeDtypeStruct((copies, rows, width), BF16),
            jax.ShapeDtypeStruct(gate.shape, BF16),
            jax.ShapeDtypeStruct(up.shape, BF16),
        ),
        in_specs=[HBM] * len(operands),
        out_specs=(VMEM,) * 4,
        scratch_shapes=[
            pltpu.SMEM((rows,), jnp.int32),
            pltpu.VMEM((rows, width), BF16),
            pltpu.VMEM((rows, head), BF16),
            pltpu.VMEM((rows, head), BF16),
            pltpu.VMEM((rows, width), BF16),
            pltpu.VMEM((rows, cache_len, head), BF16),
            pltpu.VMEM((rows, cache_len, head), BF16),
            pltpu.VMEM((rows, group, head), F32),
            pltpu.VMEM((rows, group, cache_len), BF16),
            pltpu.VMEM((rows, group, head), F32),
            pltpu.SemaphoreType.DMA((5,)),
            pltpu.SemaphoreType.DMA((2, rows)),
            pltpu.SemaphoreType.DMA((2,)),
        ],
        compiler_params=pltpu.CompilerParams(vmem_limit_bytes=24 << 20),
        cost_estimate=pl.CostEstimate(
            flops=4 * rows * group * cache_len * head,
            bytes_accessed=4 * rows * cache_len * head,
            transcendentals=rows * group * cache_len,
        ),
        name="attention",
    )(*(in_hbm(x) for x in operands))


def feed_forward_kernel(batch, tensor, place, pieces, gain, *refs):
    mate, (own_gate, own_up, down_hbm) = refs[:3], refs[3:6]
    out, normed, own_down, sems = refs[6:]
    rows, width = pieces.shape[1:]
    units, features = own_gate.shape
    role = lax.axis_index("role")

    def slot(chip):
        return place[chip] + role * (len(place) - 1 - 2 * place[chip])

    arrivals = []
    for i, start in enumerate(range(0, features, STEP)):
        span = pl.ds(start, STEP)
        arrivals.append(
            pltpu.make_async_copy(down_hbm.at[:, span], own_down.at[:, span], sems.at[i])
        )
        arrivals[-1].start()
    lanes = gain.shape[1]
    tiles = width // lanes

    for pair in range(batch // 2):
        inverse = []
        for half in range(2):
            total = jnp.zeros((rows, width), F32)
            for t in range(tensor):
                part = pieces[slot((pair * 2 + half) * tensor + t)].astype(F32)
                total = total + part * part
            mean_square = jnp.sum(total, axis=-1, keepdims=True) * (1.0 / features)
            inverse.append(lax.rsqrt(mean_square + 1e-05))
        for t in range(tensor):
            scale = jnp.concatenate(
                [gain[t * tiles + i : t * tiles + i + 1, :].astype(F32) for i in range(tiles)],
                axis=1,
            )
            parts = [
                pieces[slot((pair * 2 + half) * tensor + t)].astype(F32) * inverse[half] * scale
                for half in range(2)
            ]
            normed[pair * 2 * rows : (pair + 1) * 2 * rows, t * width : (t + 1) * width] = (
                jnp.concatenate(parts, axis=0).astype(BF16)
            )

    def project(weights):
        sums = [jnp.zeros((units, batch * rows), F32) for _ in range(2)]
        for start in range(0, features, STEP):
            span = slice(start, start + STEP)
            block = normed[:, span]
            for i in range(2):
                sums[i] += lax.dot_general(
                    weights[i][:, span], block, CONTRACT_LAST, preferred_element_type=F32
                )
        gate, up = sums
        return (gate / (1.0 + jnp.exp(-gate)) * up).astype(BF16).T

    active = jnp.concatenate([project((own_gate, own_up)), project(mate[:2])], axis=1)
    for one, start in zip(arrivals, range(0, features, STEP)):
        span = slice(start, start + STEP)
        one.wait()
        partial = jnp.dot(
            active,
            jnp.concatenate([own_down[:, span], mate[2][:, span]], axis=0),
            preferred_element_type=F32,
        )
        for i in range(STEP // width):
            t = start // width + i
            for b in range(batch):
                out[slot(b * tensor + t)] = partial[
                    b * rows : (b + 1) * rows, i * width : (i + 1) * width
                ].astype(BF16)


def feed_forward(pieces, gain, own, mate, batch, tensor, place):
    rows, width = pieces.shape[1:]
    features = tensor * width
    units = own[2].shape[0]
    return pl.pallas_call(
        functools.partial(feed_forward_kernel, batch, tensor, place),
        out_shape=jax.ShapeDtypeStruct(pieces.shape, BF16),
        in_specs=[VMEM] * 7 + [HBM],
        out_specs=VMEM,
        scratch_shapes=[
            pltpu.VMEM((batch * rows, features), BF16),
            pltpu.VMEM((units, features), BF16),
            pltpu.SemaphoreType.DMA((features // STEP,)),
        ],
        compiler_params=pltpu.CompilerParams(vmem_limit_bytes=16 << 20),
        cost_estimate=pl.CostEstimate(
            flops=12 * batch * rows * units * features,
            bytes_accessed=12 * units * features,
            transcendentals=2 * batch * rows * units,
        ),
        name="feed_forward",
    )(pieces, gain.reshape(features // 128, 128), *mate, own[0], own[1], in_hbm(own[2]))


def chip_order(batch, tensor):
    chips = batch * tensor
    side = round(chips ** (1 / 3))
    half = side // 2
    order = []
    for step in range(chips):
        at = 21 * step % chips
        z, y, x = at % side, at // side % side, at // (side * side)
        order.append((y % half * side + x) * tensor + z * half + y // half)
    return order


def local(
    queries,
    new_keys,
    new_values,
    key_cache,
    value_cache,
    lengths,
    residual,
    norm_gain,
    gate_weight,
    up_weight,
    down_weight,
):
    batch = lax.axis_size("batch")
    tensor = lax.axis_size("tensor")
    chips = batch * tensor
    order = chip_order(batch, tensor)
    place = [order.index(chip) for chip in range(chips)]
    groups = [order, [chips + chip for chip in reversed(order)]]
    exchange = functools.partial(
        lax.all_to_all,
        axis_name=AXES,
        split_axis=0,
        concat_axis=0,
        tiled=True,
        axis_index_groups=groups,
    )
    own = (gate_weight.T, up_weight.T, down_weight)
    mate = tuple(lax.ppermute(w, "role", [(0, 1), (1, 0)]) for w in own)
    hidden_state, copies, *near = attention(
        queries,
        new_keys,
        new_values,
        key_cache,
        value_cache,
        lengths,
        residual,
        chips,
        own[0],
        own[1],
    )
    pieces = exchange(copies)
    own = (*near, own[2])
    partial_out = feed_forward(pieces, norm_gain, own, mate, batch, tensor, place)
    received = exchange(partial_out)
    summed = jnp.sum(received.astype(F32), axis=0)
    return (hidden_state.astype(F32) + summed).astype(BF16)


def solution(mesh):
    rows = ("role", "batch")
    in_specs = (
        P(rows, "tensor"),
        P(rows, "tensor"),
        P(rows, "tensor"),
        P(rows, "tensor", None, None),
        P(rows, "tensor", None, None),
        P(rows),
        P(rows, "tensor"),
        P(),
        P(None, AXES),
        P(None, AXES),
        P(AXES, None),
    )
    return jax.shard_map(
        local, mesh=mesh, in_specs=in_specs, out_specs=P(rows, "tensor"), check_vma=False
    )
```

```python
import functools

import jax
import jax.numpy as jnp
from jax import lax
from jax.experimental import pallas as pl
from jax.experimental.pallas import tpu as pltpu
from jax.sharding import PartitionSpec as P

AXES = ("role", "batch", "tensor")
CHIPS = ("batch", "tensor")
PACK = 16
TOGETHER = 4
STAGE_AFTER = 0
STEP = 4096
CONTRACT_LAST = (((1,), (1,)), ((), ()))
F32 = jnp.float32
BF16 = jnp.bfloat16
HBM = pl.BlockSpec(memory_space=pltpu.HBM)
VMEM = pl.BlockSpec(memory_space=pltpu.VMEM)


def in_hbm(array):
    return pltpu.with_memory_space_constraint(array, pltpu.HBM)


def attention_kernel(
    lengths_hbm,
    queries_hbm,
    new_keys_hbm,
    new_values_hbm,
    residual_hbm,
    keys_hbm,
    values_hbm,
    gate_hbm,
    up_hbm,
    hidden_out,
    copies_out,
    gate_out,
    up_out,
    lengths,
    queries,
    new_keys,
    new_values,
    residual,
    keys,
    values,
    heads,
    probs,
    mixed,
    small_sems,
    sems,
    stage_sems,
):
    rows, group, head = heads.shape
    cache_len = keys.shape[1]
    copies = copies_out.shape[0]

    def copy(which, row):
        source, target = ((keys_hbm, keys), (values_hbm, values))[which]
        length = (lengths[row] + PACK - 1) // PACK * PACK
        span = pl.ds(0, pl.multiple_of(length, PACK))
        return pltpu.make_async_copy(
            source.at[row, 0, span], target.at[row, span], sems.at[which, row]
        )

    small = [
        pltpu.make_async_copy(source, target, small_sems.at[i])
        for i, (source, target) in enumerate(
            (
                (lengths_hbm, lengths),
                (queries_hbm, queries),
                (new_keys_hbm, new_keys),
                (new_values_hbm, new_values),
                (residual_hbm, residual),
            )
        )
    ]
    for one in small:
        one.start()
    for row in range(rows):
        values[row] = jnp.zeros((cache_len, head), BF16)
    small[0].wait()
    for which in range(2):
        for row in range(rows):
            copy(which, row).start()
    for one in small[1:]:
        one.wait()

    staged = [
        pltpu.make_async_copy(gate_hbm, gate_out, stage_sems.at[0]),
        pltpu.make_async_copy(up_hbm, up_out, stage_sems.at[1]),
    ]
    factor = head ** (-0.5)
    for j in range(group):
        heads[:, j, :] = queries[:, j * head : (j + 1) * head].astype(F32)
    own_scores = (
        jnp.sum(heads[...] * new_keys[...].astype(F32)[:, None, :], axis=-1, keepdims=True)
        * factor
    )
    place = lax.broadcasted_iota(jnp.int32, (group, cache_len), 1)
    own_probs = []
    for first in range(0, rows, TOGETHER):
        for row in range(first, first + TOGETHER):
            copy(0, row).wait()
        if first == STAGE_AFTER:
            for one in staged:
                one.start()
        for row in range(first, first + TOGETHER):
            products = lax.dot_general(
                heads[row].astype(BF16), keys[row], CONTRACT_LAST, preferred_element_type=F32
            )
            scores = jnp.where(place < lengths[row], products * factor, -jnp.inf)
            own = own_scores[row]
            top = jnp.maximum(jnp.max(scores, axis=-1, keepdims=True), own)
            weights = jnp.exp(scores - top)
            own_weight = jnp.exp(own - top)
            denominator = jnp.sum(weights, axis=-1, keepdims=True) + own_weight
            probs[row] = (weights / denominator).astype(BF16)
            own_probs.append((own_weight / denominator).astype(BF16).astype(F32))

    for first in range(0, rows, TOGETHER):
        for row in range(first, first + TOGETHER):
            copy(1, row).wait()
        for row in range(first, first + TOGETHER):
            total = own_probs[row] * new_values[row : row + 1, :].astype(F32)
            total += jnp.dot(probs[row], values[row], preferred_element_type=F32)
            mixed[row] = total

    for j in range(group):
        span = slice(j * head, (j + 1) * head)
        hidden = (residual[:, span].astype(F32) + mixed[:, j, :]).astype(BF16)
        hidden_out[:, span] = hidden
        for k in range(copies):
            copies_out[k, :, span] = hidden
    for one in staged:
        one.wait()


def attention(
    queries,
    new_keys,
    new_values,
    key_cache,
    value_cache,
    lengths,
    residual,
    copies,
    gate,
    up,
):
    rows, width = queries.shape
    head = new_keys.shape[1]
    group = width // head
    cache_len = key_cache.shape[2]
    operands = (
        lengths,
        queries,
        new_keys,
        new_values,
        residual,
        key_cache,
        value_cache,
        gate,
        up,
    )
    return pl.pallas_call(
        attention_kernel,
        out_shape=(
            jax.ShapeDtypeStruct((rows, width), BF16),
            jax.ShapeDtypeStruct((copies, rows, width), BF16),
            jax.ShapeDtypeStruct(gate.shape, BF16),
            jax.ShapeDtypeStruct(up.shape, BF16),
        ),
        in_specs=[HBM] * len(operands),
        out_specs=(VMEM,) * 4,
        scratch_shapes=[
            pltpu.SMEM((rows,), jnp.int32),
            pltpu.VMEM((rows, width), BF16),
            pltpu.VMEM((rows, head), BF16),
            pltpu.VMEM((rows, head), BF16),
            pltpu.VMEM((rows, width), BF16),
            pltpu.VMEM((rows, cache_len, head), BF16),
            pltpu.VMEM((rows, cache_len, head), BF16),
            pltpu.VMEM((rows, group, head), F32),
            pltpu.VMEM((rows, group, cache_len), BF16),
            pltpu.VMEM((rows, group, head), F32),
            pltpu.SemaphoreType.DMA((5,)),
            pltpu.SemaphoreType.DMA((2, rows)),
            pltpu.SemaphoreType.DMA((2,)),
        ],
        compiler_params=pltpu.CompilerParams(vmem_limit_bytes=24 << 20),
        cost_estimate=pl.CostEstimate(
            flops=4 * rows * group * cache_len * head,
            bytes_accessed=4 * rows * cache_len * head,
            transcendentals=rows * group * cache_len,
        ),
        name="attention",
    )(*(in_hbm(x) for x in operands))


def feed_forward_kernel(batch, tensor, place, pieces, gain, *refs):
    mate, (own_gate, own_up, down_hbm) = refs[:3], refs[3:6]
    out, own_down, turned, sems = refs[6:]
    rows, width = pieces.shape[1:]
    units, features = own_gate.shape
    role = lax.axis_index("role")

    def slot(chip):
        return place[chip] + role * (len(place) - 1 - 2 * place[chip])

    arrivals = []
    for i, start in enumerate(range(0, features, STEP)):
        span = pl.ds(start, STEP)
        arrivals.append(
            pltpu.make_async_copy(down_hbm.at[:, span], own_down.at[:, span], sems.at[i])
        )
        arrivals[-1].start()
    lanes = gain.shape[1]
    tiles = width // lanes

    inverse = []
    for b in range(batch):
        total = jnp.zeros((rows, width), F32)
        for t in range(tensor):
            part = pieces[slot(b * tensor + t)].astype(F32)
            total = total + part * part
        mean_square = jnp.sum(total, axis=-1, keepdims=True) * (1.0 / features)
        inverse.append(lax.rsqrt(mean_square + 1e-05))
    for t in range(tensor):
        scale = jnp.concatenate(
            [gain[t * tiles + i : t * tiles + i + 1, :].astype(F32) for i in range(tiles)],
            axis=1,
        )
        parts = [
            pieces[slot(b * tensor + t)].astype(F32) * inverse[b] * scale for b in range(batch)
        ]
        normed = jnp.concatenate(parts, axis=0).astype(BF16)
        turned[t * width : (t + 1) * width, :] = normed.T

    def project(weights):
        sums = [jnp.zeros((units, batch * rows), F32) for _ in range(2)]
        for start in range(0, features, STEP):
            span = slice(start, start + STEP)
            block = turned[span, :]
            for i in range(2):
                sums[i] += jnp.dot(weights[i][:, span], block, preferred_element_type=F32)
        gate, up = sums
        return (gate / (1.0 + jnp.exp(-gate)) * up).astype(BF16).T

    active = jnp.concatenate([project((own_gate, own_up)), project(mate[:2])], axis=1)
    for one, start in zip(arrivals, range(0, features, STEP)):
        span = slice(start, start + STEP)
        one.wait()
        partial = jnp.dot(
            active,
            jnp.concatenate([own_down[:, span], mate[2][:, span]], axis=0),
            preferred_element_type=F32,
        )
        for i in range(STEP // width):
            t = start // width + i
            for b in range(batch):
                out[slot(b * tensor + t)] = partial[
                    b * rows : (b + 1) * rows, i * width : (i + 1) * width
                ].astype(BF16)


def feed_forward(pieces, gain, own, mate, batch, tensor, place):
    rows, width = pieces.shape[1:]
    features = tensor * width
    units = own[2].shape[0]
    return pl.pallas_call(
        functools.partial(feed_forward_kernel, batch, tensor, place),
        out_shape=jax.ShapeDtypeStruct(pieces.shape, BF16),
        in_specs=[VMEM] * 7 + [HBM],
        out_specs=VMEM,
        scratch_shapes=[
            pltpu.VMEM((units, features), BF16),
            pltpu.VMEM((features, batch * rows), BF16),
            pltpu.SemaphoreType.DMA((features // STEP,)),
        ],
        compiler_params=pltpu.CompilerParams(vmem_limit_bytes=16 << 20),
        cost_estimate=pl.CostEstimate(
            flops=12 * batch * rows * units * features,
            bytes_accessed=12 * units * features,
            transcendentals=2 * batch * rows * units,
        ),
        name="feed_forward",
    )(pieces, gain.reshape(features // 128, 128), *mate, own[0], own[1], in_hbm(own[2]))


def chip_order(batch, tensor):
    chips = batch * tensor
    side = round(chips ** (1 / 3))
    half = side // 2
    order = []
    for step in range(chips):
        at = 21 * step % chips
        z, y, x = at % side, at // side % side, at // (side * side)
        order.append((y % half * side + x) * tensor + z * half + y // half)
    return order


def local(
    queries,
    new_keys,
    new_values,
    key_cache,
    value_cache,
    lengths,
    residual,
    norm_gain,
    gate_weight,
    up_weight,
    down_weight,
):
    batch = lax.axis_size("batch")
    tensor = lax.axis_size("tensor")
    chips = batch * tensor
    order = chip_order(batch, tensor)
    place = [order.index(chip) for chip in range(chips)]
    groups = [order, [chips + chip for chip in reversed(order)]]
    exchange = functools.partial(
        lax.all_to_all,
        axis_name=AXES,
        split_axis=0,
        concat_axis=0,
        tiled=True,
        axis_index_groups=groups,
    )
    own = (gate_weight.T, up_weight.T, down_weight)
    mate = tuple(lax.ppermute(w, "role", [(0, 1), (1, 0)]) for w in own)
    hidden_state, copies, *near = attention(
        queries,
        new_keys,
        new_values,
        key_cache,
        value_cache,
        lengths,
        residual,
        chips,
        own[0],
        own[1],
    )
    pieces = exchange(copies)
    own = (*near, own[2])
    partial_out = feed_forward(pieces, norm_gain, own, mate, batch, tensor, place)
    received = exchange(partial_out)
    summed = jnp.sum(received.astype(F32), axis=0)
    return (hidden_state.astype(F32) + summed).astype(BF16)


def solution(mesh):
    rows = ("role", "batch")
    in_specs = (
        P(rows, "tensor"),
        P(rows, "tensor"),
        P(rows, "tensor"),
        P(rows, "tensor", None, None),
        P(rows, "tensor", None, None),
        P(rows),
        P(rows, "tensor"),
        P(),
        P(None, AXES),
        P(None, AXES),
        P(AXES, None),
    )
    return jax.shard_map(
        local, mesh=mesh, in_specs=in_specs, out_specs=P(rows, "tensor"), check_vma=False
    )
```

```python
import functools

import jax
import jax.numpy as jnp
from jax import lax
from jax.experimental import pallas as pl
from jax.experimental.pallas import tpu as pltpu
from jax.sharding import PartitionSpec as P

AXES = ("role", "batch", "tensor")
CHIPS = ("batch", "tensor")
PACK = 16
TOGETHER = 8
WHOLE = 3
STAGE_AFTER = 0
STEP = 4096
CONTRACT_LAST = (((1,), (1,)), ((), ()))
F32 = jnp.float32
BF16 = jnp.bfloat16
HBM = pl.BlockSpec(memory_space=pltpu.HBM)
VMEM = pl.BlockSpec(memory_space=pltpu.VMEM)


def in_hbm(array):
    return pltpu.with_memory_space_constraint(array, pltpu.HBM)


def attention_kernel(
    lengths_hbm,
    queries_hbm,
    new_keys_hbm,
    new_values_hbm,
    residual_hbm,
    keys_hbm,
    values_hbm,
    gate_hbm,
    up_hbm,
    hidden_out,
    copies_out,
    gate_out,
    up_out,
    lengths,
    queries,
    new_keys,
    new_values,
    residual,
    keys,
    values,
    heads,
    probs,
    mixed,
    small_sems,
    sems,
    stage_sems,
):
    rows, group, head = heads.shape
    cache_len = keys.shape[1]
    copies = copies_out.shape[0]

    def copy(which, row):
        source, target = ((keys_hbm, keys), (values_hbm, values))[which]
        if which == 0 and row < WHOLE:
            span = pl.ds(0, cache_len)
        else:
            length = (lengths[row] + PACK - 1) // PACK * PACK
            span = pl.ds(0, pl.multiple_of(length, PACK))
        return pltpu.make_async_copy(
            source.at[row, 0, span], target.at[row, span], sems.at[which, row]
        )

    small = [
        pltpu.make_async_copy(source, target, small_sems.at[i])
        for i, (source, target) in enumerate(
            (
                (lengths_hbm, lengths),
                (queries_hbm, queries),
                (new_keys_hbm, new_keys),
                (new_values_hbm, new_values),
                (residual_hbm, residual),
            )
        )
    ]
    for one in small:
        one.start()
    for row in range(WHOLE):
        copy(0, row).start()
    for row in range(rows):
        values[row] = jnp.zeros((cache_len, head), BF16)
    small[0].wait()
    for which in range(2):
        for row in range(rows):
            if which or row >= WHOLE:
                copy(which, row).start()
    for one in small[1:]:
        one.wait()

    staged = [
        pltpu.make_async_copy(gate_hbm, gate_out, stage_sems.at[0]),
        pltpu.make_async_copy(up_hbm, up_out, stage_sems.at[1]),
    ]
    factor = head ** (-0.5)
    for j in range(group):
        heads[:, j, :] = queries[:, j * head : (j + 1) * head].astype(F32)
    own_scores = (
        jnp.sum(heads[...] * new_keys[...].astype(F32)[:, None, :], axis=-1, keepdims=True)
        * factor
    )
    place = lax.broadcasted_iota(jnp.int32, (group, cache_len), 1)
    own_probs = []
    for first, last in ((0, WHOLE), (WHOLE, rows)):
        for row in range(first, last):
            copy(0, row).wait()
        if first == STAGE_AFTER:
            for one in staged:
                one.start()
        for row in range(first, last):
            products = lax.dot_general(
                heads[row].astype(BF16), keys[row], CONTRACT_LAST, preferred_element_type=F32
            )
            scores = jnp.where(place < lengths[row], products * factor, -jnp.inf)
            own = own_scores[row]
            top = jnp.maximum(jnp.max(scores, axis=-1, keepdims=True), own)
            weights = jnp.exp(scores - top)
            own_weight = jnp.exp(own - top)
            denominator = jnp.sum(weights, axis=-1, keepdims=True) + own_weight
            probs[row] = (weights / denominator).astype(BF16)
            own_probs.append((own_weight / denominator).astype(BF16).astype(F32))

    for first in range(0, rows, TOGETHER):
        for row in range(first, first + TOGETHER):
            copy(1, row).wait()
        for row in range(first, first + TOGETHER):
            total = own_probs[row] * new_values[row : row + 1, :].astype(F32)
            total += jnp.dot(probs[row], values[row], preferred_element_type=F32)
            mixed[row] = total

    for j in range(group):
        span = slice(j * head, (j + 1) * head)
        hidden = (residual[:, span].astype(F32) + mixed[:, j, :]).astype(BF16)
        hidden_out[:, span] = hidden
        for k in range(copies):
            copies_out[k, :, span] = hidden
    for one in staged:
        one.wait()


def attention(
    queries,
    new_keys,
    new_values,
    key_cache,
    value_cache,
    lengths,
    residual,
    copies,
    gate,
    up,
):
    rows, width = queries.shape
    head = new_keys.shape[1]
    group = width // head
    cache_len = key_cache.shape[2]
    operands = (
        lengths,
        queries,
        new_keys,
        new_values,
        residual,
        key_cache,
        value_cache,
        gate,
        up,
    )
    return pl.pallas_call(
        attention_kernel,
        out_shape=(
            jax.ShapeDtypeStruct((rows, width), BF16),
            jax.ShapeDtypeStruct((copies, rows, width), BF16),
            jax.ShapeDtypeStruct(gate.shape, BF16),
            jax.ShapeDtypeStruct(up.shape, BF16),
        ),
        in_specs=[HBM] * len(operands),
        out_specs=(VMEM,) * 4,
        scratch_shapes=[
            pltpu.SMEM((rows,), jnp.int32),
            pltpu.VMEM((rows, width), BF16),
            pltpu.VMEM((rows, head), BF16),
            pltpu.VMEM((rows, head), BF16),
            pltpu.VMEM((rows, width), BF16),
            pltpu.VMEM((rows, cache_len, head), BF16),
            pltpu.VMEM((rows, cache_len, head), BF16),
            pltpu.VMEM((rows, group, head), F32),
            pltpu.VMEM((rows, group, cache_len), BF16),
            pltpu.VMEM((rows, group, head), F32),
            pltpu.SemaphoreType.DMA((5,)),
            pltpu.SemaphoreType.DMA((2, rows)),
            pltpu.SemaphoreType.DMA((2,)),
        ],
        compiler_params=pltpu.CompilerParams(vmem_limit_bytes=24 << 20),
        cost_estimate=pl.CostEstimate(
            flops=4 * rows * group * cache_len * head,
            bytes_accessed=4 * rows * cache_len * head,
            transcendentals=rows * group * cache_len,
        ),
        name="attention",
    )(*(in_hbm(x) for x in operands))


def feed_forward_kernel(batch, tensor, place, pieces, gain, *refs):
    mate, (own_gate, own_up, down_hbm) = refs[:3], refs[3:6]
    out, own_down, turned, sems = refs[6:]
    rows, width = pieces.shape[1:]
    units, features = own_gate.shape
    role = lax.axis_index("role")

    def slot(chip):
        return place[chip] + role * (len(place) - 1 - 2 * place[chip])

    arrivals = []
    for i, start in enumerate(range(0, features, STEP)):
        span = pl.ds(start, STEP)
        arrivals.append(
            pltpu.make_async_copy(down_hbm.at[:, span], own_down.at[:, span], sems.at[i])
        )
        arrivals[-1].start()
    lanes = gain.shape[1]
    tiles = width // lanes

    inverse = []
    for b in range(batch):
        total = jnp.zeros((rows, width), F32)
        for t in range(tensor):
            part = pieces[slot(b * tensor + t)].astype(F32)
            total = total + part * part
        mean_square = jnp.sum(total, axis=-1, keepdims=True) * (1.0 / features)
        inverse.append(lax.rsqrt(mean_square + 1e-05))
    for t in range(tensor):
        scale = jnp.concatenate(
            [gain[t * tiles + i : t * tiles + i + 1, :].astype(F32) for i in range(tiles)],
            axis=1,
        )
        parts = [
            pieces[slot(b * tensor + t)].astype(F32) * inverse[b] * scale for b in range(batch)
        ]
        normed = jnp.concatenate(parts, axis=0).astype(BF16)
        turned[t * width : (t + 1) * width, :] = normed.T

    def project(weights):
        sums = [jnp.zeros((units, batch * rows), F32) for _ in range(2)]
        for start in range(0, features, STEP):
            span = slice(start, start + STEP)
            block = turned[span, :]
            for i in range(2):
                sums[i] += jnp.dot(weights[i][:, span], block, preferred_element_type=F32)
        gate, up = sums
        return (gate / (1.0 + jnp.exp(-gate)) * up).astype(BF16).T

    active = jnp.concatenate([project((own_gate, own_up)), project(mate[:2])], axis=1)
    for one, start in zip(arrivals, range(0, features, STEP)):
        span = slice(start, start + STEP)
        one.wait()
        partial = jnp.dot(
            active,
            jnp.concatenate([own_down[:, span], mate[2][:, span]], axis=0),
            preferred_element_type=F32,
        )
        for i in range(STEP // width):
            t = start // width + i
            for b in range(batch):
                out[slot(b * tensor + t)] = partial[
                    b * rows : (b + 1) * rows, i * width : (i + 1) * width
                ].astype(BF16)


def feed_forward(pieces, gain, own, mate, batch, tensor, place):
    rows, width = pieces.shape[1:]
    features = tensor * width
    units = own[2].shape[0]
    return pl.pallas_call(
        functools.partial(feed_forward_kernel, batch, tensor, place),
        out_shape=jax.ShapeDtypeStruct(pieces.shape, BF16),
        in_specs=[VMEM] * 7 + [HBM],
        out_specs=VMEM,
        scratch_shapes=[
            pltpu.VMEM((units, features), BF16),
            pltpu.VMEM((features, batch * rows), BF16),
            pltpu.SemaphoreType.DMA((features // STEP,)),
        ],
        compiler_params=pltpu.CompilerParams(vmem_limit_bytes=16 << 20),
        cost_estimate=pl.CostEstimate(
            flops=12 * batch * rows * units * features,
            bytes_accessed=12 * units * features,
            transcendentals=2 * batch * rows * units,
        ),
        name="feed_forward",
    )(pieces, gain.reshape(features // 128, 128), *mate, own[0], own[1], in_hbm(own[2]))


def chip_order(batch, tensor):
    chips = batch * tensor
    side = round(chips ** (1 / 3))
    half = side // 2
    order = []
    for step in range(chips):
        at = 21 * step % chips
        z, y, x = at % side, at // side % side, at // (side * side)
        order.append((y % half * side + x) * tensor + z * half + y // half)
    return order


def local(
    queries,
    new_keys,
    new_values,
    key_cache,
    value_cache,
    lengths,
    residual,
    norm_gain,
    gate_weight,
    up_weight,
    down_weight,
):
    batch = lax.axis_size("batch")
    tensor = lax.axis_size("tensor")
    chips = batch * tensor
    order = chip_order(batch, tensor)
    place = [order.index(chip) for chip in range(chips)]
    groups = [order, [chips + chip for chip in reversed(order)]]
    exchange = functools.partial(
        lax.all_to_all,
        axis_name=AXES,
        split_axis=0,
        concat_axis=0,
        tiled=True,
        axis_index_groups=groups,
    )
    own = (gate_weight.T, up_weight.T, down_weight)
    mate = tuple(lax.ppermute(w, "role", [(0, 1), (1, 0)]) for w in own)
    hidden_state, copies, *near = attention(
        queries,
        new_keys,
        new_values,
        key_cache,
        value_cache,
        lengths,
        residual,
        chips,
        own[0],
        own[1],
    )
    pieces = exchange(copies)
    own = (*near, own[2])
    partial_out = feed_forward(pieces, norm_gain, own, mate, batch, tensor, place)
    received = exchange(partial_out)
    summed = jnp.sum(received.astype(F32), axis=0)
    return (hidden_state.astype(F32) + summed).astype(BF16)


def solution(mesh):
    rows = ("role", "batch")
    in_specs = (
        P(rows, "tensor"),
        P(rows, "tensor"),
        P(rows, "tensor"),
        P(rows, "tensor", None, None),
        P(rows, "tensor", None, None),
        P(rows),
        P(rows, "tensor"),
        P(),
        P(None, AXES),
        P(None, AXES),
        P(AXES, None),
    )
    return jax.shard_map(
        local, mesh=mesh, in_specs=in_specs, out_specs=P(rows, "tensor"), check_vma=False
    )
```

```python
import functools

import jax
import jax.numpy as jnp
from jax import lax
from jax.experimental import pallas as pl
from jax.experimental.pallas import tpu as pltpu
from jax.sharding import PartitionSpec as P

AXES = ("role", "batch", "tensor")
CHIPS = ("batch", "tensor")
PACK = 16
TOGETHER = 8
WHOLE = 3
STAGE_AFTER = 0
STEP = 4096
CONTRACT_LAST = (((1,), (1,)), ((), ()))
F32 = jnp.float32
BF16 = jnp.bfloat16
HBM = pl.BlockSpec(memory_space=pltpu.HBM)
VMEM = pl.BlockSpec(memory_space=pltpu.VMEM)


def in_hbm(array):
    return pltpu.with_memory_space_constraint(array, pltpu.HBM)


def attention_kernel(
    lengths_hbm,
    queries_hbm,
    new_keys_hbm,
    new_values_hbm,
    residual_hbm,
    keys_hbm,
    values_hbm,
    gate_hbm,
    up_hbm,
    hidden_out,
    copies_out,
    gate_out,
    up_out,
    lengths,
    queries,
    new_keys,
    new_values,
    residual,
    keys,
    values,
    heads,
    probs,
    mixed,
    small_sems,
    sems,
    stage_sems,
):
    rows, group, head = heads.shape
    cache_len = keys.shape[1]
    copies = copies_out.shape[0]

    def copy(which, row):
        source, target = ((keys_hbm, keys), (values_hbm, values))[which]
        if which == 0 and row < WHOLE:
            span = pl.ds(0, cache_len)
        else:
            length = (lengths[row] + PACK - 1) // PACK * PACK
            span = pl.ds(0, pl.multiple_of(length, PACK))
        return pltpu.make_async_copy(
            source.at[row, 0, span], target.at[row, span], sems.at[which, row]
        )

    small = [
        pltpu.make_async_copy(source, target, small_sems.at[i])
        for i, (source, target) in enumerate(
            (
                (lengths_hbm, lengths),
                (queries_hbm, queries),
                (new_keys_hbm, new_keys),
                (new_values_hbm, new_values),
                (residual_hbm, residual),
            )
        )
    ]
    for one in small:
        one.start()
    for row in range(WHOLE):
        copy(0, row).start()
    half = rows // 2
    for row in range(half):
        values[row] = jnp.zeros((cache_len, head), BF16)
    small[0].wait()
    for row in range(WHOLE, rows):
        copy(0, row).start()
    for row in range(half):
        copy(1, row).start()
    for row in range(half, rows):
        values[row] = jnp.zeros((cache_len, head), BF16)
        copy(1, row).start()
    for one in small[1:]:
        one.wait()

    staged = [
        pltpu.make_async_copy(gate_hbm, gate_out, stage_sems.at[0]),
        pltpu.make_async_copy(up_hbm, up_out, stage_sems.at[1]),
    ]
    factor = head ** (-0.5)
    for j in range(group):
        heads[:, j, :] = queries[:, j * head : (j + 1) * head].astype(F32)
    own_scores = (
        jnp.sum(heads[...] * new_keys[...].astype(F32)[:, None, :], axis=-1, keepdims=True)
        * factor
    )
    place = lax.broadcasted_iota(jnp.int32, (group, cache_len), 1)
    own_probs = []
    for first, last in ((0, WHOLE), (WHOLE, rows)):
        for row in range(first, last):
            copy(0, row).wait()
        if first == STAGE_AFTER:
            for one in staged:
                one.start()
        for row in range(first, last):
            products = lax.dot_general(
                heads[row].astype(BF16), keys[row], CONTRACT_LAST, preferred_element_type=F32
            )
            scores = jnp.where(place < lengths[row], products * factor, -jnp.inf)
            own = own_scores[row]
            top = jnp.maximum(jnp.max(scores, axis=-1, keepdims=True), own)
            weights = jnp.exp(scores - top)
            own_weight = jnp.exp(own - top)
            denominator = jnp.sum(weights, axis=-1, keepdims=True) + own_weight
            probs[row] = (weights / denominator).astype(BF16)
            own_probs.append((own_weight / denominator).astype(BF16).astype(F32))

    for first in range(0, rows, TOGETHER):
        for row in range(first, first + TOGETHER):
            copy(1, row).wait()
        for row in range(first, first + TOGETHER):
            total = own_probs[row] * new_values[row : row + 1, :].astype(F32)
            total += jnp.dot(probs[row], values[row], preferred_element_type=F32)
            mixed[row] = total

    for j in range(group):
        span = slice(j * head, (j + 1) * head)
        hidden = (residual[:, span].astype(F32) + mixed[:, j, :]).astype(BF16)
        hidden_out[:, span] = hidden
        for k in range(copies):
            copies_out[k, :, span] = hidden
    for one in staged:
        one.wait()


def attention(
    queries,
    new_keys,
    new_values,
    key_cache,
    value_cache,
    lengths,
    residual,
    copies,
    gate,
    up,
):
    rows, width = queries.shape
    head = new_keys.shape[1]
    group = width // head
    cache_len = key_cache.shape[2]
    operands = (
        lengths,
        queries,
        new_keys,
        new_values,
        residual,
        key_cache,
        value_cache,
        gate,
        up,
    )
    return pl.pallas_call(
        attention_kernel,
        out_shape=(
            jax.ShapeDtypeStruct((rows, width), BF16),
            jax.ShapeDtypeStruct((copies, rows, width), BF16),
            jax.ShapeDtypeStruct(gate.shape, BF16),
            jax.ShapeDtypeStruct(up.shape, BF16),
        ),
        in_specs=[HBM] * len(operands),
        out_specs=(VMEM,) * 4,
        scratch_shapes=[
            pltpu.SMEM((rows,), jnp.int32),
            pltpu.VMEM((rows, width), BF16),
            pltpu.VMEM((rows, head), BF16),
            pltpu.VMEM((rows, head), BF16),
            pltpu.VMEM((rows, width), BF16),
            pltpu.VMEM((rows, cache_len, head), BF16),
            pltpu.VMEM((rows, cache_len, head), BF16),
            pltpu.VMEM((rows, group, head), F32),
            pltpu.VMEM((rows, group, cache_len), BF16),
            pltpu.VMEM((rows, group, head), F32),
            pltpu.SemaphoreType.DMA((5,)),
            pltpu.SemaphoreType.DMA((2, rows)),
            pltpu.SemaphoreType.DMA((2,)),
        ],
        compiler_params=pltpu.CompilerParams(vmem_limit_bytes=24 << 20),
        cost_estimate=pl.CostEstimate(
            flops=4 * rows * group * cache_len * head,
            bytes_accessed=4 * rows * cache_len * head,
            transcendentals=rows * group * cache_len,
        ),
        name="attention",
    )(*(in_hbm(x) for x in operands))


def feed_forward_kernel(batch, tensor, place, pieces, gain, *refs):
    mate, (own_gate, own_up, down_hbm) = refs[:3], refs[3:6]
    out, own_down, turned, sems = refs[6:]
    rows, width = pieces.shape[1:]
    units, features = own_gate.shape
    role = lax.axis_index("role")

    def slot(chip):
        return place[chip] + role * (len(place) - 1 - 2 * place[chip])

    arrivals = []
    for i, start in enumerate(range(0, features, STEP)):
        span = pl.ds(start, STEP)
        arrivals.append(
            pltpu.make_async_copy(down_hbm.at[:, span], own_down.at[:, span], sems.at[i])
        )
        arrivals[-1].start()
    lanes = gain.shape[1]
    tiles = width // lanes

    inverse = []
    for b in range(batch):
        total = jnp.zeros((rows, width), F32)
        for t in range(tensor):
            part = pieces[slot(b * tensor + t)].astype(F32)
            total = total + part * part
        mean_square = jnp.sum(total, axis=-1, keepdims=True) * (1.0 / features)
        inverse.append(lax.rsqrt(mean_square + 1e-05))
    for t in range(tensor):
        scale = jnp.concatenate(
            [gain[t * tiles + i : t * tiles + i + 1, :].astype(F32) for i in range(tiles)],
            axis=1,
        )
        parts = [
            pieces[slot(b * tensor + t)].astype(F32) * inverse[b] * scale for b in range(batch)
        ]
        normed = jnp.concatenate(parts, axis=0).astype(BF16)
        turned[t * width : (t + 1) * width, :] = normed.T

    projections = (own_gate, own_up, mate[0], mate[1])
    sums = [jnp.zeros((units, batch * rows), F32) for _ in projections]
    for start in range(0, features, STEP):
        span = slice(start, start + STEP)
        block = turned[span, :]
        for i, w in enumerate(projections):
            sums[i] += jnp.dot(w[:, span], block, preferred_element_type=F32)
    active = jnp.concatenate(
        [
            (gate / (1.0 + jnp.exp(-gate)) * up).astype(BF16).T
            for gate, up in (sums[:2], sums[2:])
        ],
        axis=1,
    )
    for one, start in zip(arrivals, range(0, features, STEP)):
        span = slice(start, start + STEP)
        one.wait()
        partial = jnp.dot(
            active,
            jnp.concatenate([own_down[:, span], mate[2][:, span]], axis=0),
            preferred_element_type=F32,
        )
        for i in range(STEP // width):
            t = start // width + i
            for b in range(batch):
                out[slot(b * tensor + t)] = partial[
                    b * rows : (b + 1) * rows, i * width : (i + 1) * width
                ].astype(BF16)


def feed_forward(pieces, gain, own, mate, batch, tensor, place):
    rows, width = pieces.shape[1:]
    features = tensor * width
    units = own[2].shape[0]
    return pl.pallas_call(
        functools.partial(feed_forward_kernel, batch, tensor, place),
        out_shape=jax.ShapeDtypeStruct(pieces.shape, BF16),
        in_specs=[VMEM] * 7 + [HBM],
        out_specs=VMEM,
        scratch_shapes=[
            pltpu.VMEM((units, features), BF16),
            pltpu.VMEM((features, batch * rows), BF16),
            pltpu.SemaphoreType.DMA((features // STEP,)),
        ],
        compiler_params=pltpu.CompilerParams(vmem_limit_bytes=16 << 20),
        cost_estimate=pl.CostEstimate(
            flops=12 * batch * rows * units * features,
            bytes_accessed=12 * units * features,
            transcendentals=2 * batch * rows * units,
        ),
        name="feed_forward",
    )(pieces, gain.reshape(features // 128, 128), *mate, own[0], own[1], in_hbm(own[2]))


def chip_order(batch, tensor):
    chips = batch * tensor
    side = round(chips ** (1 / 3))
    half = side // 2
    order = []
    for step in range(chips):
        at = 21 * step % chips
        z, y, x = at % side, at // side % side, at // (side * side)
        order.append((y % half * side + x) * tensor + z * half + y // half)
    return order


def local(
    queries,
    new_keys,
    new_values,
    key_cache,
    value_cache,
    lengths,
    residual,
    norm_gain,
    gate_weight,
    up_weight,
    down_weight,
):
    batch = lax.axis_size("batch")
    tensor = lax.axis_size("tensor")
    chips = batch * tensor
    order = chip_order(batch, tensor)
    place = [order.index(chip) for chip in range(chips)]
    groups = [order, [chips + chip for chip in reversed(order)]]
    exchange = functools.partial(
        lax.all_to_all,
        axis_name=AXES,
        split_axis=0,
        concat_axis=0,
        tiled=True,
        axis_index_groups=groups,
    )
    own = (gate_weight.T, up_weight.T, down_weight)
    mate = tuple(lax.ppermute(w, "role", [(0, 1), (1, 0)]) for w in own)
    hidden_state, copies, *near = attention(
        queries,
        new_keys,
        new_values,
        key_cache,
        value_cache,
        lengths,
        residual,
        chips,
        own[0],
        own[1],
    )
    pieces = exchange(copies)
    own = (*near, own[2])
    partial_out = feed_forward(pieces, norm_gain, own, mate, batch, tensor, place)
    received = exchange(partial_out)
    total = hidden_state.astype(F32)
    for chip in range(chips):
        total += received[chip].astype(F32)
    return total.astype(BF16)


def solution(mesh):
    rows = ("role", "batch")
    in_specs = (
        P(rows, "tensor"),
        P(rows, "tensor"),
        P(rows, "tensor"),
        P(rows, "tensor", None, None),
        P(rows, "tensor", None, None),
        P(rows),
        P(rows, "tensor"),
        P(),
        P(None, AXES),
        P(None, AXES),
        P(AXES, None),
    )
    return jax.shard_map(
        local, mesh=mesh, in_specs=in_specs, out_specs=P(rows, "tensor"), check_vma=False
    )
```

```python
import functools

import jax
import jax.numpy as jnp
from jax import lax
from jax.experimental import pallas as pl
from jax.experimental.pallas import tpu as pltpu
from jax.sharding import PartitionSpec as P

AXES = ("role", "batch", "tensor")
CHIPS = ("batch", "tensor")
PACK = 16
TOGETHER = 8
WHOLE = 3
STAGE_AFTER = 0
STEP = 4096
CONTRACT_LAST = (((1,), (1,)), ((), ()))
F32 = jnp.float32
BF16 = jnp.bfloat16
HBM = pl.BlockSpec(memory_space=pltpu.HBM)
VMEM = pl.BlockSpec(memory_space=pltpu.VMEM)


def in_hbm(array):
    return pltpu.with_memory_space_constraint(array, pltpu.HBM)


def attention_kernel(
    lengths_hbm,
    queries_hbm,
    new_keys_hbm,
    new_values_hbm,
    residual_hbm,
    keys_hbm,
    values_hbm,
    gate_hbm,
    up_hbm,
    hidden_out,
    copies_out,
    gate_out,
    up_out,
    lengths,
    queries,
    new_keys,
    new_values,
    residual,
    keys,
    values,
    heads,
    probs,
    mixed,
    small_sems,
    sems,
    stage_sems,
):
    rows, group, head = heads.shape
    cache_len = keys.shape[1]
    copies = copies_out.shape[0]

    def copy(which, row):
        source, target = ((keys_hbm, keys), (values_hbm, values))[which]
        if which == 0 and row < WHOLE:
            span = pl.ds(0, cache_len)
        else:
            length = (lengths[row] + PACK - 1) // PACK * PACK
            span = pl.ds(0, pl.multiple_of(length, PACK))
        return pltpu.make_async_copy(
            source.at[row, 0, span], target.at[row, span], sems.at[which, row]
        )

    small = [
        pltpu.make_async_copy(source, target, small_sems.at[i])
        for i, (source, target) in enumerate(
            (
                (lengths_hbm, lengths),
                (queries_hbm, queries),
                (new_keys_hbm, new_keys),
                (new_values_hbm, new_values),
                (residual_hbm, residual),
            )
        )
    ]
    for one in small:
        one.start()
    for row in range(WHOLE):
        copy(0, row).start()
    half = rows // 2
    for row in range(half):
        values[row] = jnp.zeros((cache_len, head), BF16)
    small[0].wait()
    for row in range(WHOLE, rows):
        copy(0, row).start()
    for row in range(half):
        copy(1, row).start()
    for row in range(half, rows):
        values[row] = jnp.zeros((cache_len, head), BF16)
        copy(1, row).start()
    for one in small[1:]:
        one.wait()

    staged = [
        pltpu.make_async_copy(gate_hbm, gate_out, stage_sems.at[0]),
        pltpu.make_async_copy(up_hbm, up_out, stage_sems.at[1]),
    ]
    factor = head ** (-0.5)
    for j in range(group):
        heads[:, j, :] = queries[:, j * head : (j + 1) * head].astype(F32)
    own_scores = (
        jnp.sum(heads[...] * new_keys[...].astype(F32)[:, None, :], axis=-1, keepdims=True)
        * factor
    )
    place = lax.broadcasted_iota(jnp.int32, (group, cache_len), 1)
    own_probs = []
    for first, last in ((0, WHOLE), (WHOLE, rows)):
        for row in range(first, last):
            copy(0, row).wait()
        if first == STAGE_AFTER:
            for one in staged:
                one.start()
        for row in range(first, last):
            products = lax.dot_general(
                heads[row].astype(BF16), keys[row], CONTRACT_LAST, preferred_element_type=F32
            )
            scores = jnp.where(place < lengths[row], products * factor, -jnp.inf)
            own = own_scores[row]
            top = jnp.maximum(jnp.max(scores, axis=-1, keepdims=True), own)
            weights = jnp.exp(scores - top)
            own_weight = jnp.exp(own - top)
            denominator = jnp.sum(weights, axis=-1, keepdims=True) + own_weight
            probs[row] = (weights / denominator).astype(BF16)
            own_probs.append((own_weight / denominator).astype(BF16).astype(F32))

    for first in range(0, rows, TOGETHER):
        for row in range(first, first + TOGETHER):
            copy(1, row).wait()
        for row in range(first, first + TOGETHER):
            total = own_probs[row] * new_values[row : row + 1, :].astype(F32)
            total += jnp.dot(probs[row], values[row], preferred_element_type=F32)
            mixed[row] = total

    for j in range(group):
        span = slice(j * head, (j + 1) * head)
        hidden = (residual[:, span].astype(F32) + mixed[:, j, :]).astype(BF16)
        hidden_out[:, span] = hidden
        for k in range(copies):
            copies_out[k, :, span] = hidden
    for one in staged:
        one.wait()


def attention(
    queries,
    new_keys,
    new_values,
    key_cache,
    value_cache,
    lengths,
    residual,
    copies,
    gate,
    up,
):
    rows, width = queries.shape
    head = new_keys.shape[1]
    group = width // head
    cache_len = key_cache.shape[2]
    operands = (
        lengths,
        queries,
        new_keys,
        new_values,
        residual,
        key_cache,
        value_cache,
        gate,
        up,
    )
    return pl.pallas_call(
        attention_kernel,
        out_shape=(
            jax.ShapeDtypeStruct((rows, width), BF16),
            jax.ShapeDtypeStruct((copies, rows, width), BF16),
            jax.ShapeDtypeStruct(gate.shape, BF16),
            jax.ShapeDtypeStruct(up.shape, BF16),
        ),
        in_specs=[HBM] * len(operands),
        out_specs=(VMEM,) * 4,
        scratch_shapes=[
            pltpu.SMEM((rows,), jnp.int32),
            pltpu.VMEM((rows, width), BF16),
            pltpu.VMEM((rows, head), BF16),
            pltpu.VMEM((rows, head), BF16),
            pltpu.VMEM((rows, width), BF16),
            pltpu.VMEM((rows, cache_len, head), BF16),
            pltpu.VMEM((rows, cache_len, head), BF16),
            pltpu.VMEM((rows, group, head), F32),
            pltpu.VMEM((rows, group, cache_len), BF16),
            pltpu.VMEM((rows, group, head), F32),
            pltpu.SemaphoreType.DMA((5,)),
            pltpu.SemaphoreType.DMA((2, rows)),
            pltpu.SemaphoreType.DMA((2,)),
        ],
        compiler_params=pltpu.CompilerParams(vmem_limit_bytes=24 << 20),
        cost_estimate=pl.CostEstimate(
            flops=4 * rows * group * cache_len * head,
            bytes_accessed=4 * rows * cache_len * head,
            transcendentals=rows * group * cache_len,
        ),
        name="attention",
    )(*(in_hbm(x) for x in operands))


def feed_forward_kernel(batch, tensor, place, pieces, gain, *refs):
    mate, (own_gate, own_up, down_hbm) = refs[:3], refs[3:6]
    out, own_down, turned, sems = refs[6:]
    rows, width = pieces.shape[1:]
    units, features = own_gate.shape
    role = lax.axis_index("role")

    def slot(chip):
        return place[chip] + role * (len(place) - 1 - 2 * place[chip])

    arrivals = []
    for i, start in enumerate(range(0, features, STEP)):
        span = pl.ds(start, STEP)
        arrivals.append(
            pltpu.make_async_copy(down_hbm.at[:, span], own_down.at[:, span], sems.at[i])
        )
        arrivals[-1].start()
    lanes = gain.shape[1]
    tiles = width // lanes

    inverse = []
    for b in range(batch):
        total = jnp.zeros((rows, width), F32)
        for t in range(tensor):
            part = pieces[slot(b * tensor + t)].astype(F32)
            total = total + part * part
        mean_square = jnp.sum(total, axis=-1, keepdims=True) * (1.0 / features)
        inverse.append(lax.rsqrt(mean_square + 1e-05))
    for t in range(tensor):
        scale = jnp.concatenate(
            [gain[t * tiles + i : t * tiles + i + 1, :].astype(F32) for i in range(tiles)],
            axis=1,
        )
        parts = [
            pieces[slot(b * tensor + t)].astype(F32) * inverse[b] * scale for b in range(batch)
        ]
        normed = jnp.concatenate(parts, axis=0).astype(BF16)
        turned[t * width : (t + 1) * width, :] = normed.T

    projections = (own_gate, own_up, mate[0], mate[1])
    sums = [jnp.zeros((units, batch * rows), F32) for _ in projections]
    for start in range(0, features, STEP):
        span = slice(start, start + STEP)
        block = turned[span, :]
        for i, w in enumerate(projections):
            sums[i] += jnp.dot(w[:, span], block, preferred_element_type=F32)
    active = jnp.concatenate(
        [
            (gate / (1.0 + jnp.exp(-gate)) * up).astype(BF16).T
            for gate, up in (sums[:2], sums[2:])
        ],
        axis=1,
    )
    for one, start in zip(arrivals, range(0, features, STEP)):
        span = slice(start, start + STEP)
        one.wait()
        partial = jnp.dot(
            active,
            jnp.concatenate([own_down[:, span], mate[2][:, span]], axis=0),
            preferred_element_type=F32,
        )
        for i in range(STEP // width):
            t = start // width + i
            for b in range(batch):
                out[slot(b * tensor + t)] = partial[
                    b * rows : (b + 1) * rows, i * width : (i + 1) * width
                ].astype(BF16)


def feed_forward(pieces, gain, own, mate, batch, tensor, place):
    rows, width = pieces.shape[1:]
    features = tensor * width
    units = own[2].shape[0]
    return pl.pallas_call(
        functools.partial(feed_forward_kernel, batch, tensor, place),
        out_shape=jax.ShapeDtypeStruct(pieces.shape, BF16),
        in_specs=[VMEM] * 7 + [HBM],
        out_specs=VMEM,
        scratch_shapes=[
            pltpu.VMEM((units, features), BF16),
            pltpu.VMEM((features, batch * rows), BF16),
            pltpu.SemaphoreType.DMA((features // STEP,)),
        ],
        compiler_params=pltpu.CompilerParams(vmem_limit_bytes=16 << 20),
        cost_estimate=pl.CostEstimate(
            flops=12 * batch * rows * units * features,
            bytes_accessed=12 * units * features,
            transcendentals=2 * batch * rows * units,
        ),
        name="feed_forward",
    )(pieces, gain.reshape(features // 128, 128), *mate, own[0], own[1], in_hbm(own[2]))


def chip_order(batch, tensor):
    chips = batch * tensor
    side = round(chips ** (1 / 3))
    half = side // 2
    order = []
    for step in range(chips):
        at = 21 * step % chips
        y, z, x = at % side, at // side % side, at // (side * side)
        order.append((y % half * side + x) * tensor + z * half + y // half)
    return order


def local(
    queries,
    new_keys,
    new_values,
    key_cache,
    value_cache,
    lengths,
    residual,
    norm_gain,
    gate_weight,
    up_weight,
    down_weight,
):
    batch = lax.axis_size("batch")
    tensor = lax.axis_size("tensor")
    chips = batch * tensor
    order = chip_order(batch, tensor)
    place = [order.index(chip) for chip in range(chips)]
    groups = [order, [chips + chip for chip in reversed(order)]]
    exchange = functools.partial(
        lax.all_to_all,
        axis_name=AXES,
        split_axis=0,
        concat_axis=0,
        tiled=True,
        axis_index_groups=groups,
    )
    own = (gate_weight.T, up_weight.T, down_weight)
    mate = tuple(lax.ppermute(w, "role", [(0, 1), (1, 0)]) for w in own)
    hidden_state, copies, *near = attention(
        queries,
        new_keys,
        new_values,
        key_cache,
        value_cache,
        lengths,
        residual,
        chips,
        own[0],
        own[1],
    )
    pieces = exchange(copies)
    own = (*near, own[2])
    partial_out = feed_forward(pieces, norm_gain, own, mate, batch, tensor, place)
    received = exchange(partial_out)
    total = hidden_state.astype(F32)
    for chip in range(chips):
        total += received[chip].astype(F32)
    return total.astype(BF16)


def solution(mesh):
    rows = ("role", "batch")
    in_specs = (
        P(rows, "tensor"),
        P(rows, "tensor"),
        P(rows, "tensor"),
        P(rows, "tensor", None, None),
        P(rows, "tensor", None, None),
        P(rows),
        P(rows, "tensor"),
        P(),
        P(None, AXES),
        P(None, AXES),
        P(AXES, None),
    )
    return jax.shard_map(
        local, mesh=mesh, in_specs=in_specs, out_specs=P(rows, "tensor"), check_vma=False
    )
```
